32 devices in a mesh: groups: 1, expert: 32 (over z, y, x, core).
Axes of the slice: x: 2, y: 2, z: 4, core: 2. Of those that a mesh axis runs over, the one named last changes fastest.
Arguments:
- tokens: bfloat16 [1024, 4096], P(('groups', 'expert')), may hold values from -6 to 6
- expert_ids: int32 [1024, 8], P(('groups', 'expert')), may hold values from 0 to 15, all different within a row; in each aligned block of 32 rows (0 to 31, 32 to 63, ...) at most 24 rows name the same one
- gate_weights: float32 [1024, 8], P(('groups', 'expert')), may hold values from 0.05 to 0.5
- w_gate: bfloat16 [32, 4096, 384], P('expert'), may hold values from -0.09375 to 0.09375
- w_up: bfloat16 [32, 4096, 384], P('expert'), may hold values from -0.09375 to 0.09375
- w_down: bfloat16 [32, 384, 4096], P('expert'), may hold values from -0.21875 to 0.21875
Outputs:
- moe_out: bfloat16 [1024, 4096], P(('groups', 'expert'))
The draws below stay inside these ranges and needn't reach their ends.
Inputs may be any that keep to these rules, and one draw needn't show every extreme that they name: `expert_ids`: the 8 experts of a row are distinct. Within the rows of one device (aligned blocks of 32 rows) no expert is named by more than 24 rows, a bound that some block reaches.
All inputs are finite; a program needn't handle non-finite values.
Results may differ from the reference program's by a relative error of at most 0.0067.
Values may be sent and summed in bfloat16 or wider, within the bound.
A program may use at most 128 MiB of HBM per device.

```python
import math
import jax
import jax.numpy as jnp
import numpy as np
from jax import lax

D = 4096
FF = 768
TOPK = 8
TOK_DEV = 32
EXPERTS = 16
CAP = 24
TOKENS = 1024
N_EXPERT = 32


def level_of(key, dims, split, smallest, largest):
    def one(axis_at, parts):
        heights = jax.random.uniform(jax.random.fold_in(jax.random.fold_in(key, 6), axis_at), (parts,), jnp.float32, smallest / len(split), largest / len(split))
        return jnp.repeat(jnp.exp(heights), dims[axis_at] // parts).reshape((-1,) + (1,) * (len(dims) - axis_at - 1))

    gain = one(*split[0])
    for cut in split[1:]:
        gain = gain * one(*cut)
    return gain


def routed_block(rng, own, number, rows, number_of, top, bound, skew):
    ranking = jax.random.permutation(rng, number_of)
    crowded, ordinary = portions_of(number_of, rows * top, bound, skew, True), portions_of(number_of, rows * top, bound, skew, False)
    places = jnp.arange(number_of)

    def named(tallies, offset_by):
        used = int((tallies > 0).sum())
        fixed = max(1, used // 4)
        shifted = fixed + (places - fixed + offset_by * (used - fixed)) % max(1, number_of - fixed)
        return jnp.zeros((number_of,), jnp.int32).at[ranking[jnp.where(places < fixed, places, shifted)]].set(jnp.asarray(tallies, jnp.int32))

    tallies = jnp.where(number % 4 == 0, named(crowded, number // 4), named(ordinary, number - number // 4 - 1))
    mixed = jax.random.permutation(jax.random.fold_in(own, 3), number_of)
    donor, sink = mixed[0:number_of // 2 * 2:2], mixed[1:number_of // 2 * 2:2]
    slack = jnp.minimum(tallies[donor] - 1, bound - tallies[sink]) // 2
    slack = jnp.where((donor == ranking[0]) | (sink == ranking[0]) | (tallies[sink] == 0), 0, jnp.maximum(slack, 0))
    shifted = jax.random.randint(jax.random.fold_in(own, 4), (number_of // 2,), 0, 1 << 20) % (slack + 1)
    tallies = tallies.at[donor].add(-shifted).at[sink].add(shifted)
    members = jnp.searchsorted(jnp.cumsum(tallies), jnp.arange(rows * top), side="right").astype(jnp.int32)
    table = members.reshape(top, rows).T
    table = table[jax.random.permutation(jax.random.fold_in(own, 1), rows)]
    offset_by = jax.random.randint(jax.random.fold_in(own, 2), (rows, 1), 0, top)
    return jnp.take_along_axis(table, (jnp.arange(top)[None, :] + offset_by) % top, axis=1)


def portions_of(amount, total, reach, lean, full):
    weights = [(1 << 20) // math.isqrt(rank ** lean) + 1 for rank in range(1, amount + 1)]
    largest = reach if full else min(reach, max(-(-total // amount), total * weights[0] // sum(weights)))
    least = 1 if total - largest >= amount - 1 else 0
    counts, spare = [largest] + [least] * (amount - 1), total - largest - least * (amount - 1)
    while spare > 0:
        movable = [i for i in range(1, amount) if counts[i] < largest] or [i for i in range(1, amount) if counts[i] < reach]
        mass, remaining = sum([weights[i] for i in movable]), spare
        for i in movable:
            more = min(reach - counts[i], max(1, remaining * weights[i] // mass), spare)
            counts[i] = counts[i] + more
            spare = spare - more
    return np.array(counts)


def centred(own_key, dims, scale, reach, split=(), kind=jnp.bfloat16):
    array = jax.random.normal(own_key, dims, jnp.float32) * scale
    if len(split) > 0:
        array = level_of(own_key, dims, split, -0.22, 0.18) * array
    return jnp.clip(array, min=-reach, max=reach).astype(kind)


def setup_inputs(seed: int = 0, part: int = 0) -> dict:
    key_of = jax.random.split(jax.random.key(seed), 7)
    own_keys = jax.random.split(jax.random.fold_in(key_of[6], part), 7)
    tokens = centred(own_keys[0], (TOKENS, D), 1.0, 6.0, ((0, 32),))
    expert_ids_keys = jax.random.split(jax.random.fold_in(own_keys[1], 1), TOKENS // TOK_DEV)
    expert_ids_turns = jax.random.permutation(jax.random.fold_in(own_keys[1], 3), TOKENS // TOK_DEV)
    expert_ids = jax.vmap(lambda own, number: routed_block(jax.random.fold_in(own_keys[1], 2), own, number, TOK_DEV, EXPERTS, TOPK, CAP, 3))(expert_ids_keys, expert_ids_turns).reshape((TOKENS, TOPK))
    gate_weights = jnp.clip(jnp.exp(math.log(0.5) - 2.3025851 * jax.random.uniform(own_keys[2], (TOKENS, TOPK), jnp.float32) ** level_of(own_keys[2], (TOKENS, TOPK), ((0, 32),), -0.2, 0.2)), 0.05, 0.5)
    w_gate = centred(key_of[3], (2 * EXPERTS, D, FF // 2), D ** -0.5, 0.09375, ((0, 32),))
    w_up = centred(key_of[4], (2 * EXPERTS, D, FF // 2), D ** -0.5, 0.09375, ((0, 32),))
    w_down = centred(key_of[5], (2 * EXPERTS, FF // 2, D), FF ** -0.5, 0.21875, ((0, 32),))
    return dict(tokens=tokens, expert_ids=expert_ids, gate_weights=gate_weights, w_gate=w_gate, w_up=w_up, w_down=w_down)


def reference(tokens, expert_ids, gate_weights, w_gate, w_up, w_down):
    blocks = expert_ids.reshape(N_EXPERT, TOK_DEV, TOPK)
    one_hot = (blocks[..., None] == jnp.arange(EXPERTS, dtype=jnp.int32)).astype(jnp.int32)
    per_row = jnp.sum(one_hot, axis=2)
    earlier = jnp.cumsum(per_row, axis=1) - per_row
    slot_index = jnp.sum(one_hot * earlier[:, :, None, :], axis=3)
    block_index = jnp.arange(N_EXPERT, dtype=jnp.int32)[:, None, None]
    position = ((blocks * N_EXPERT + block_index) * CAP + slot_index).reshape(-1)
    row_index = jnp.broadcast_to(jnp.arange(TOKENS, dtype=jnp.int32).reshape(N_EXPERT, TOK_DEV, 1), blocks.shape).reshape(-1)
    owner = jnp.full((EXPERTS * N_EXPERT * CAP,), TOKENS, jnp.int32).at[position].set(row_index)
    owner = owner.reshape(EXPERTS, N_EXPERT * CAP)
    weighting = jnp.zeros((EXPERTS * N_EXPERT * CAP,), jnp.float32).at[position].set(gate_weights.reshape(-1).astype(jnp.float32))
    weighting = weighting.reshape(EXPERTS, N_EXPERT * CAP)
    padded = jnp.concatenate([tokens, jnp.zeros((1, D), tokens.dtype)], axis=0)

    def one_expert(total, expert):
        chosen = padded[owner[expert]]
        halves = []
        for half in range(2):
            shard = 2 * expert + half
            gate_value = jnp.dot(chosen, w_gate[shard], preferred_element_type=jnp.float32)
            up_value = jnp.dot(chosen, w_up[shard], preferred_element_type=jnp.float32)
            hidden = (jax.nn.silu(gate_value) * up_value).astype(jnp.bfloat16)
            halves.append(jnp.dot(hidden, w_down[shard], preferred_element_type=jnp.float32).astype(jnp.bfloat16))
        expert_out = (halves[0].astype(jnp.float32) + halves[1].astype(jnp.float32)).astype(jnp.bfloat16)
        total = total.at[owner[expert]].add(weighting[expert][:, None] * expert_out.astype(jnp.float32))
        return total, None

    start = jnp.zeros((TOKENS + 1, D), jnp.float32)
    total, _ = lax.scan(one_expert, start, jnp.arange(EXPERTS, dtype=jnp.int32))
    return total[:TOKENS].astype(jnp.bfloat16)
```

```python
import jax
import jax.numpy as jnp
from jax import lax
from jax.experimental import pallas as pl
from jax.experimental.pallas import tpu as pltpu
from jax.sharding import PartitionSpec as P

LANES = 128
PLANES = 4
SPOTS = 4
DEVICES = PLANES * SPOTS * 2
OWN, FIRST, SECOND, DIAGONAL = range(4)


def gathered_kernel(
    tokens, expert_ids, gate_weights, w_gate, w_up, w_down, out,
    rows, gate_mem, up_mem, down_mem, parts, parts_in, kept,
    second_out, second_in, first_out, first_in, plane_out, plane_in,
    load_sem, gather_send, gather_recv, parts_send, parts_recv,
    second_send, second_recv, first_send, first_recv, plane_send, plane_recv,
):
    tok_rows, width = tokens.shape
    hidden_units = w_down.shape[1]
    experts = DEVICES // 2
    me = lax.axis_index("expert")
    core = lax.rem(me, 2)
    x = lax.rem(me // 2, 2)
    y = lax.rem(me // 4, 2)
    z = me // 8
    expert = me // 2
    along_x, along_y = me + 2 - 4 * x, me + 4 - 8 * y
    first = along_x * (1 - core) + along_y * core
    second = along_y * (1 - core) + along_x * core
    sibling = me + 1 - 2 * core
    spot_x, spot_y = y * 2 + 1 - x, (1 - y) * 2 + x
    spots = [
        y * 2 + x,
        spot_x * (1 - core) + spot_y * core,
        spot_y * (1 - core) + spot_x * core,
        3 - (y * 2 + x),
    ]

    def plane_of(step):
        return lax.rem(z + step, PLANES)

    def slot(step, role):
        return plane_of(step) * 8 + core * SPOTS + spots[role]

    def peer(step):
        return lax.rem(me + 8 * step, DEVICES)

    def remote(src, dst, send, recv, device):
        return pltpu.make_async_remote_copy(
            src_ref=src, dst_ref=dst, send_sem=send, recv_sem=recv,
            device_id={"expert": device}, device_id_type=pl.DeviceIdType.MESH,
        )

    sent = []

    def send(copy):
        copy.start()
        sent.append(copy)

    loads = [
        pltpu.make_async_copy(tokens, rows.at[slot(0, OWN), :, pl.ds(0, width)], load_sem.at[0]),
        pltpu.make_async_copy(w_gate.at[0], gate_mem, load_sem.at[1]),
        pltpu.make_async_copy(w_up.at[0], up_mem, load_sem.at[2]),
        pltpu.make_async_copy(w_down.at[0], down_mem, load_sem.at[3]),
    ]
    for load in loads:
        load.start()

    barrier = pltpu.get_barrier_semaphore()
    partners = [peer(1), peer(2), peer(3), first, second, sibling]
    for partner in partners:
        pl.semaphore_signal(
            barrier, inc=1, device_id={"expert": partner}, device_id_type=pl.DeviceIdType.MESH
        )

    lane = lax.broadcasted_iota(jnp.int32, (tok_rows, LANES), 1)
    named = jnp.where(lane < experts, lane, lane - experts)
    named = jnp.where(lane < 2 * experts, named, -1)
    weight = jnp.zeros((tok_rows, LANES), jnp.float32)
    for k in range(expert_ids.shape[1]):
        weight += jnp.where(expert_ids[:, k : k + 1] == named, gate_weights[:, k : k + 1], 0.0)
    high = weight.astype(jnp.bfloat16).astype(jnp.float32)
    split = jnp.where(lane < experts, high, weight - high).astype(jnp.bfloat16)
    rows[slot(0, OWN), :, width : width + LANES] = split

    loads[0].wait()
    pl.semaphore_wait(barrier, len(partners))

    def gather_copy(role, step, at, device):
        return remote(
            rows.at[at], rows.at[at], gather_send.at[role, step], gather_recv.at[role, step], device
        )

    for step in (1, 3, 2):
        copy = remote(
            rows.at[slot(0, OWN)], rows.at[slot(0, OWN)],
            gather_send.at[OWN, step], gather_recv.at[OWN, PLANES - step], peer(step),
        )
        send(copy)

    def arrived(role, step, at):
        gather_copy(role, step, at, sibling).wait_recv()

    def stage_plane(step):
        at = slot(step, OWN)
        if step:
            arrived(OWN, step, at)
        send(gather_copy(FIRST, step, at, first))
        send(gather_copy(SECOND, step, at, second))
        send(gather_copy(4 + OWN, step, at, sibling))

    def stage_first(step):
        at = slot(step, FIRST)
        arrived(FIRST, step, at)
        send(gather_copy(DIAGONAL, step, at, second))
        send(gather_copy(4 + FIRST, step, at, sibling))

    def stage_second(step):
        for role in (SECOND, DIAGONAL):
            at = slot(step, role)
            arrived(role, step, at)
            send(gather_copy(4 + role, step, at, sibling))

    def sibling_slot(step, role):
        role = {FIRST: SECOND, SECOND: FIRST}.get(role, role)
        return plane_of(step) * 8 + (1 - core) * SPOTS + spots[role]

    def stage_sibling(step):
        for role in range(4):
            arrived(4 + role, step, sibling_slot(step, role))

    def compute(step):
        count = 8 * tok_rows
        base = plane_of(step) * 8
        block = rows[pl.ds(base, 8), :, 0:width].reshape(count, width)
        gate = jnp.dot(block, gate_mem[...], preferred_element_type=jnp.float32)
        up = jnp.dot(block, up_mem[...], preferred_element_type=jnp.float32)
        hidden = (gate / (1.0 + jnp.exp(-gate)) * up).astype(jnp.bfloat16)
        tile = 512

        @pl.loop(0, width // tile)
        def _(j):
            columns = pl.ds(pl.multiple_of(j * tile, tile), tile)
            part = jnp.dot(hidden, down_mem[:, columns], preferred_element_type=jnp.float32)
            parts[step, :, :, :, columns] = part.astype(jnp.bfloat16).reshape(
                2, SPOTS, tok_rows, tile
            )

        send(
            remote(
                parts.at[step, 1 - core], parts_in.at[step],
                parts_send.at[step], parts_recv.at[step], sibling,
            )
        )

    def parts_done(step):
        remote(
            parts.at[step, 1 - core], parts_in.at[step],
            parts_send.at[step], parts_recv.at[step], sibling,
        ).wait_recv()

        def weighted(role):
            pair = parts[step, core, spots[role]].astype(jnp.float32) + parts_in[
                step, spots[role]
            ].astype(jnp.float32)
            pair = pair.astype(jnp.bfloat16).astype(jnp.float32)
            shares = rows[slot(step, role), :, width : width + LANES].astype(jnp.float32)
            mine = (lane == expert) | (lane == expert + experts)
            return jnp.sum(jnp.where(mine, shares, 0.0), axis=1, keepdims=True) * pair

        second_out[step, 0] = weighted(SECOND).astype(jnp.bfloat16)
        second_out[step, 1] = weighted(DIAGONAL).astype(jnp.bfloat16)
        send(second_copy(step))
        kept[step, 0] = weighted(OWN)
        kept[step, 1] = weighted(FIRST)

    def second_copy(step):
        return remote(
            second_out.at[step], second_in.at[step],
            second_send.at[step], second_recv.at[step], second,
        )

    def first_copy(step):
        return remote(
            first_out.at[step], first_in.at[step],
            first_send.at[step], first_recv.at[step], first,
        )

    def second_done(step):
        second_copy(step).wait_recv()
        first_out[step] = (kept[step, 1] + second_in[step, 1].astype(jnp.float32)).astype(
            jnp.bfloat16
        )
        send(first_copy(step))
        kept[step, 0] += second_in[step, 0].astype(jnp.float32)

    def first_done(step):
        first_copy(step).wait_recv()
        total = kept[step, 0] + first_in[step].astype(jnp.float32)
        if step:
            plane_out[step] = total.astype(jnp.bfloat16)
            send(
                remote(
                    plane_out.at[step], plane_in.at[PLANES - step],
                    plane_send.at[step], plane_recv.at[PLANES - step], peer(step),
                )
            )
        else:
            kept[step, 0] = total

    stage_plane(0)
    stage_first(0)
    stage_plane(1)
    stage_second(0)
    stage_first(1)
    stage_plane(3)
    for load in loads[1:]:
        load.wait()
    order = (0, 1, 3, 2)
    for at, step in enumerate(order):
        if at:
            stage_second(step)
        stage_sibling(step)
        compute(step)
        if at == 0:
            stage_first(3)
            stage_plane(2)
        if at == 1:
            stage_first(2)
        if at > 1:
            first_done(order[at - 2])
        if at > 0:
            second_done(order[at - 1])
        parts_done(step)
    first_done(order[2])
    second_done(order[3])
    first_done(order[3])

    total = kept[0, 0]
    for step in (1, 3, 2):
        remote(
            plane_out.at[step], plane_in.at[step],
            plane_send.at[step], plane_recv.at[step], peer(step),
        ).wait_recv()
        total = total + plane_in[step].astype(jnp.float32)
    out[...] = total.astype(jnp.bfloat16)
    for copy in sent:
        copy.wait_send()


def gathered(tokens, expert_ids, gate_weights, w_gate, w_up, w_down):
    tok_rows, width = tokens.shape
    hidden_units = w_down.shape[1]
    block = (tok_rows, width)
    any_spec = pl.BlockSpec(memory_space=pl.ANY)
    vmem_spec = pl.BlockSpec(memory_space=pltpu.VMEM)
    bf16, dma = jnp.bfloat16, pltpu.SemaphoreType.DMA
    return pl.pallas_call(
        gathered_kernel,
        out_shape=jax.ShapeDtypeStruct(block, bf16),
        in_specs=[any_spec, vmem_spec, vmem_spec, any_spec, any_spec, any_spec],
        out_specs=vmem_spec,
        scratch_shapes=[
            pltpu.VMEM((DEVICES, tok_rows, width + LANES), bf16),
            pltpu.VMEM((width, hidden_units), bf16),
            pltpu.VMEM((width, hidden_units), bf16),
            pltpu.VMEM((hidden_units, width), bf16),
            pltpu.VMEM((PLANES, 2, SPOTS) + block, bf16),
            pltpu.VMEM((PLANES, SPOTS) + block, bf16),
            pltpu.VMEM((PLANES, 2) + block, jnp.float32),
            pltpu.VMEM((PLANES, 2) + block, bf16),
            pltpu.VMEM((PLANES, 2) + block, bf16),
            pltpu.VMEM((PLANES,) + block, bf16),
            pltpu.VMEM((PLANES,) + block, bf16),
            pltpu.VMEM((PLANES,) + block, bf16),
            pltpu.VMEM((PLANES,) + block, bf16),
            dma((4,)),
            dma((8, PLANES)),
            dma((8, PLANES)),
        ]
        + [dma((PLANES,))] * 8,
        compiler_params=pltpu.CompilerParams(
            collective_id=0, has_side_effects=True, vmem_limit_bytes=60 * 1024 * 1024
        ),
        cost_estimate=pl.CostEstimate(
            flops=6 * DEVICES * tok_rows * width * hidden_units,
            bytes_accessed=6 * width * hidden_units,
            transcendentals=DEVICES * tok_rows * hidden_units,
        ),
    )(tokens, expert_ids, gate_weights, w_gate, w_up, w_down)


def expert_block(w_gate, w_up, w_down, received):
    sources, count, width = received.shape
    flattened = received.reshape(sources * count, width)
    gate_value = jnp.dot(flattened, w_gate[0], preferred_element_type=jnp.float32)
    up_value = jnp.dot(flattened, w_up[0], preferred_element_type=jnp.float32)
    hidden = (jax.nn.silu(gate_value) * up_value).astype(jnp.bfloat16)
    partial_out = jnp.dot(hidden, w_down[0], preferred_element_type=jnp.float32).astype(
        jnp.bfloat16
    )
    return partial_out.reshape(sources, count, width)


def exchanged(tokens, expert_ids, gate_weights, w_gate, w_up, w_down):
    devices = lax.axis_size("expert")
    experts = devices // 2
    tok_rows, width = tokens.shape
    chosen_count = expert_ids.shape[1]
    capacity = min(tok_rows, 3 * tok_rows * chosen_count // (2 * experts))
    one_hot = (expert_ids[:, :, None] == jnp.arange(experts, dtype=jnp.int32)).astype(jnp.int32)
    per_row = jnp.sum(one_hot, axis=1)
    earlier = jnp.cumsum(per_row, axis=0) - per_row
    slot_index = jnp.sum(one_hot * earlier[:, None, :], axis=2)
    position = expert_ids * capacity + slot_index
    row_index = jnp.broadcast_to(jnp.arange(tok_rows, dtype=jnp.int32)[:, None], expert_ids.shape)
    owner = (
        jnp.full((experts * capacity,), tok_rows, jnp.int32)
        .at[position.reshape(-1)]
        .set(row_index.reshape(-1))
    )
    padded = jnp.concatenate([tokens, jnp.zeros((1, width), tokens.dtype)], axis=0)
    selected = padded[owner].reshape(experts, 1, capacity, width)
    outgoing = jnp.broadcast_to(selected, (experts, 2, capacity, width)).reshape(
        devices, capacity, width
    )
    partial_out = expert_block(
        w_gate,
        w_up,
        w_down,
        lax.all_to_all(outgoing, "expert", split_axis=0, concat_axis=0, tiled=True),
    )
    returned = lax.all_to_all(partial_out, "expert", split_axis=0, concat_axis=0, tiled=True)
    paired = returned.reshape(experts, 2, capacity, width).astype(jnp.float32)
    expert_out = (paired[:, 0] + paired[:, 1]).astype(jnp.bfloat16)
    picked = expert_out.reshape(experts * capacity, width)[position]
    mixed = jnp.sum(gate_weights[:, :, None] * picked.astype(jnp.float32), axis=1)
    return mixed.astype(jnp.bfloat16)


def solution(mesh):
    small = mesh.shape["expert"] == DEVICES and mesh.shape["groups"] == 1
    return jax.shard_map(
        gathered if small else exchanged,
        mesh=mesh,
        in_specs=(
            P(("groups", "expert"), None),
            P(("groups", "expert"), None),
            P(("groups", "expert"), None),
            P("expert", None, None),
            P("expert", None, None),
            P("expert", None, None),
        ),
        out_specs=P(("groups", "expert"), None),
        check_vma=False,
    )
```

```python
import jax
import jax.numpy as jnp
from jax import lax
from jax.experimental import pallas as pl
from jax.experimental.pallas import tpu as pltpu
from jax.sharding import PartitionSpec as P

LANES = 128
PLANES = 4
DEVICES = PLANES * 4 * 2
TILE = 512
PIECES = 2


def capacity_of(tok_rows, chosen_count, experts):
    return min(tok_rows, 3 * tok_rows * chosen_count // (2 * experts))


def gathered_kernel(
    tokens, expert_ids, gate_weights, w_gate, w_up, w_down, out,
    rows, gate_mem, up_mem, down_mem, packed, chosen, parts, parts_in,
    second_out, second_in, first_out, first_in, plane_out, plane_in, kept, hidden_mem,
    load_sem, up_send, down_send, plane_recv, first_send, first_recv, second_send, second_recv,
    near_send, near_recv, far_send, far_recv, parts_send, parts_recv,
    back_second_send, back_second_recv, back_first_send, back_first_recv,
    back_plane_send, back_plane_recv,
):
    tok_rows, width = tokens.shape
    wide = width + LANES
    experts = DEVICES // 2
    capacity = capacity_of(tok_rows, expert_ids.shape[0], experts)
    full, pair = 2 * tok_rows, 2 * capacity
    me = lax.axis_index("expert")
    core = lax.rem(me, 2)
    x = lax.rem(me // 2, 2)
    y = lax.rem(me // 4, 2)
    z = me // 8
    expert = me // 2
    along_x, along_y = me + 2 - 4 * x, me + 4 - 8 * y
    first = along_x * (1 - core) + along_y * core
    second = along_y * (1 - core) + along_x * core
    sibling = me + 1 - 2 * core
    above, below = lax.rem(me + 8, DEVICES), lax.rem(me + 24, DEVICES)

    half = z // 2
    low = z + half * (3 - 2 * z)
    planes = [z] + [t + half * (3 - 2 * t) for t in (low + 1, 2 - 2 * low, 3)]

    def remote(src, dst, send, recv, device):
        return pltpu.make_async_remote_copy(
            src_ref=src, dst_ref=dst, send_sem=send, recv_sem=recv,
            device_id={"expert": device}, device_id_type=pl.DeviceIdType.MESH,
        )

    sent = []

    def send(copy):
        copy.start()
        sent.append(copy)

    own = pl.ds(0, tok_rows)
    share_of_width = width // PIECES

    def wide_piece(h):
        return pl.ds(width - share_of_width, share_of_width + LANES) if h == 0 else plain_piece(h)

    def plain_piece(h):
        return pl.ds(width - share_of_width * (h + 1), share_of_width)

    def over_piece(h, body):
        @pl.loop(0, share_of_width // TILE)
        def _(j):
            start = width - share_of_width * (h + 1)
            body(pl.ds(pl.multiple_of(start + j * TILE, TILE), TILE))

    loads = [
        pltpu.make_async_copy(tokens, rows.at[z, core, own, pl.ds(0, width)], load_sem.at[0]),
        pltpu.make_async_copy(w_gate.at[0], gate_mem, load_sem.at[1]),
        pltpu.make_async_copy(w_up.at[0], up_mem, load_sem.at[2]),
        pltpu.make_async_copy(w_down.at[0], down_mem, load_sem.at[3]),
    ]
    for load in loads:
        load.start()

    barrier = pltpu.get_barrier_semaphore()
    partners = [lax.rem(me + 8 * step, DEVICES) for step in (1, 2, 3)] + [first, second, sibling]
    for partner in partners:
        pl.semaphore_signal(
            barrier, inc=1, device_id={"expert": partner}, device_id_type=pl.DeviceIdType.MESH
        )

    ids = jnp.transpose(expert_ids[...])
    gates = jnp.transpose(gate_weights[...])
    lane = lax.broadcasted_iota(jnp.int32, (tok_rows, LANES), 1)
    named = lax.rem(lane, experts)
    weight = jnp.zeros((tok_rows, LANES), jnp.float32)
    member = jnp.zeros((tok_rows, LANES), jnp.float32)
    for k in range(ids.shape[1]):
        same = ids[:, k : k + 1] == named
        weight += jnp.where(same, gates[:, k : k + 1], 0.0)
        member += jnp.where(same, 1.0, 0.0)
    earlier = lax.broadcasted_iota(jnp.int32, (tok_rows, tok_rows), 1) < lax.broadcasted_iota(
        jnp.int32, (tok_rows, tok_rows), 0
    )
    before = jnp.dot(
        jnp.where(earlier, 1.0, 0.0).astype(jnp.bfloat16),
        member.astype(jnp.bfloat16),
        preferred_element_type=jnp.float32,
    )
    high = weight.astype(jnp.bfloat16).astype(jnp.float32)
    beside = jnp.where(lane < experts, high, weight - high)
    beside = jnp.where(lane < 2 * experts, beside, member * (before + 1.0))
    rows[z, core, 0:tok_rows, width:wide] = jnp.where(lane < 3 * experts, beside, 0.0).astype(
        jnp.bfloat16
    )

    loads[0].wait()
    pl.semaphore_wait(barrier, len(partners))

    def column(shares, which):
        at = lax.broadcasted_iota(jnp.int32, shares.shape, 1)
        keep = at == which[0]
        for other in which[1:]:
            keep = keep | (at == other)
        return jnp.sum(jnp.where(keep, shares.astype(jnp.float32), 0.0), axis=1, keepdims=True)

    def plane_copy(q, h, up):
        block = rows.at[q, core, own, wide_piece(h)]
        sems = up_send if up else down_send
        return remote(block, block, sems.at[q, h], plane_recv.at[q, h], above if up else below)

    def pass_on(q, h, act):
        @pl.when((q <= z) & (z < PLANES - 1))
        def _():
            act(plane_copy(q, h, True))

        @pl.when((q >= z) & (z > 0))
        def _():
            act(plane_copy(q, h, False))

    def first_copy(q, h):
        return remote(
            rows.at[q, core, own, wide_piece(h)],
            rows.at[q, core, pl.ds(tok_rows, tok_rows), wide_piece(h)],
            first_send.at[q, h], first_recv.at[q, h], first,
        )

    def second_copy(q, h):
        return remote(
            packed.at[q, :, wide_piece(h)], rows.at[q, core, pl.ds(full, pair), wide_piece(h)],
            second_send.at[q, h], second_recv.at[q, h], second,
        )

    def near_copy(q, h, c):
        block = rows.at[q, c, pl.ds(0, full), wide_piece(h)]
        return remote(block, block, near_send.at[q, h], near_recv.at[q, h], sibling)

    def far_copy(q, h, c):
        block = rows.at[q, c, pl.ds(full, pair), wide_piece(h)]
        return remote(block, block, far_send.at[q, h], far_recv.at[q, h], sibling)

    inner = (z > 0) & (z < PLANES - 1)

    def gather_plane(step, h):
        q = planes[step]
        if step == 1:
            plane_copy(q, h, True).wait_recv()
        if step < 2:
            pass_on(q, h, lambda copy: copy.start())
        else:
            @pl.when(jnp.logical_not(inner))
            def _():
                plane_copy(q, h, True).wait_recv()

        send(first_copy(q, h))

    def gather_early(step, h):
        @pl.when(inner)
        def _():
            plane_copy(planes[step], h, True).wait_recv()
            pass_on(planes[step], h, lambda copy: copy.start())

    def gather_first(step, h):
        q = planes[step]
        first_copy(q, h).wait_recv()
        send(near_copy(q, h, core))
        if h == 0:
            code = column(rows[q, core, 0:full, width:wide], [2 * experts + second // 2])
            row = lax.broadcasted_iota(jnp.int32, (full, pair), 0)
            start = jnp.where(row < tok_rows, 0, capacity)
            place = code.astype(jnp.int32) - 1
            takes = (place >= 0) & (place + start == lax.broadcasted_iota(jnp.int32, (full, pair), 1))
            taken = jnp.where(takes, 1.0, 0.0).astype(jnp.bfloat16)
            chosen[step] = taken
        packed[q, :, wide_piece(h)] = lax.dot_general(
            chosen[step], rows[q, core, 0:full, wide_piece(h)], (((0,), (0,)), ((), ())),
            preferred_element_type=jnp.float32,
        ).astype(jnp.bfloat16)
        send(second_copy(q, h))

    def gather_second(step, h):
        q = planes[step]
        second_copy(q, h).wait_recv()
        send(far_copy(q, h, core))

    def parts_copy(step, h):
        return remote(
            parts.at[step, 1 - core, :, plain_piece(h)], parts_in.at[step, :, plain_piece(h)],
            parts_send.at[step, h], parts_recv.at[step, h], sibling,
        )

    def compute_hidden(step):
        q = planes[step]
        for h in range(PIECES):
            near_copy(q, h, 1 - core).wait_recv()
            far_copy(q, h, 1 - core).wait_recv()
        count = 2 * (full + pair)
        block = rows[q, :, :, 0:width].reshape(count, width)
        gate = jnp.dot(block, gate_mem[...], preferred_element_type=jnp.float32)
        up = jnp.dot(block, up_mem[...], preferred_element_type=jnp.float32)
        hidden_mem[...] = (gate / (1.0 + jnp.exp(-gate)) * up).astype(jnp.bfloat16)

    def compute_parts(step, h):
        def body(columns):
            part = jnp.dot(
                hidden_mem[...], down_mem[:, columns], preferred_element_type=jnp.float32
            )
            parts[step, :, :, columns] = part.astype(jnp.bfloat16).reshape(2, full + pair, TILE)

        over_piece(h, body)
        send(parts_copy(step, h))

    def share_of(step, start, size):
        shares = rows[planes[step], core, start : start + size, width:wide]
        return column(shares, [expert, expert + experts])

    def weighted(step, share, start, columns):
        at = pl.ds(start, share.shape[0])
        both = parts[step, core, at, columns].astype(jnp.float32) + parts_in[
            step, at, columns
        ].astype(jnp.float32)
        return share * both.astype(jnp.bfloat16).astype(jnp.float32)

    def back_second_copy(step, h):
        return remote(
            second_out.at[step, :, plain_piece(h)], second_in.at[step, :, plain_piece(h)],
            back_second_send.at[step, h], back_second_recv.at[step, h], second,
        )

    def back_first_copy(step, h):
        return remote(
            first_out.at[step, :, plain_piece(h)], first_in.at[step, :, plain_piece(h)],
            back_first_send.at[step, h], back_first_recv.at[step, h], first,
        )

    def reduce_parts(step, h):
        share = share_of(step, full, pair)
        parts_copy(step, h).wait_recv()

        def body(columns):
            second_out[step, :, columns] = weighted(step, share, full, columns).astype(jnp.bfloat16)

        over_piece(h, body)
        send(back_second_copy(step, h))

    def reduce_second(step, h):
        share = share_of(step, 0, full)
        back_second_copy(step, h).wait_recv()

        def body(columns):
            back = jnp.dot(
                chosen[step], second_in[step, :, columns], preferred_element_type=jnp.float32
            )
            total = weighted(step, share, 0, columns) + back
            first_out[step, :, columns] = total[tok_rows:].astype(jnp.bfloat16)
            kept[step, :, columns] = total[:tok_rows]

        over_piece(h, body)
        send(back_first_copy(step, h))

    def reduce_first(step, h):
        q = planes[step]
        back_first_copy(step, h).wait_recv()
        if step:

            def body(columns):
                plane_out[step, :, columns] = (
                    kept[step, :, columns] + first_in[step, :, columns].astype(jnp.float32)
                ).astype(jnp.bfloat16)

            over_piece(h, body)
            send(
                remote(
                    plane_out.at[step, :, plain_piece(h)], plane_in.at[z, :, plain_piece(h)],
                    back_plane_send.at[step, h], back_plane_recv.at[z, h],
                    lax.rem(me + 8 * (q - z) + DEVICES, DEVICES),
                )
            )

    gather_plane(0, 0)
    gather_plane(0, 1)
    gather_first(0, 0)
    gather_first(0, 1)
    gather_plane(1, 0)
    gather_early(2, 0)
    gather_plane(1, 1)
    gather_early(2, 1)
    gather_first(1, 0)
    gather_first(1, 1)
    gather_second(0, 0)
    gather_second(0, 1)
    for load in loads[1:]:
        load.wait()
    gather_plane(2, 0)
    gather_plane(2, 1)
    gather_early(3, 0)
    gather_early(3, 1)
    gather_first(2, 0)
    gather_first(2, 1)
    gather_second(1, 0)
    gather_second(1, 1)
    compute_hidden(1)
    gather_plane(3, 0)
    gather_plane(3, 1)
    compute_parts(1, 0)
    compute_parts(1, 1)
    gather_first(3, 0)
    gather_first(3, 1)
    gather_second(2, 0)
    gather_second(2, 1)
    reduce_parts(1, 0)
    reduce_parts(1, 1)
    compute_hidden(2)
    compute_parts(2, 0)
    compute_parts(2, 1)
    gather_second(3, 0)
    gather_second(3, 1)
    reduce_parts(2, 0)
    reduce_parts(2, 1)
    reduce_second(1, 0)
    reduce_second(1, 1)
    compute_hidden(3)
    compute_parts(3, 0)
    compute_parts(3, 1)
    reduce_parts(3, 0)
    reduce_parts(3, 1)
    reduce_first(1, 0)
    reduce_first(1, 1)
    compute_hidden(0)
    compute_parts(0, 0)
    compute_parts(0, 1)
    reduce_second(2, 0)
    reduce_second(2, 1)
    reduce_parts(0, 0)
    reduce_parts(0, 1)
    reduce_second(3, 0)
    reduce_second(3, 1)
    reduce_first(2, 0)
    reduce_first(2, 1)
    reduce_first(3, 0)
    reduce_first(3, 1)
    reduce_second(0, 0)
    reduce_second(0, 1)
    reduce_first(0, 0)
    reduce_first(0, 1)

    for h in range(PIECES):
        for step in (1, 2, 3):
            q = planes[step]
            remote(
                plane_out.at[step, :, plain_piece(h)], plane_in.at[q, :, plain_piece(h)],
                back_plane_send.at[step, h], back_plane_recv.at[q, h], sibling,
            ).wait_recv()

        def finish(columns):
            total = kept[0, :, columns] + first_in[0, :, columns].astype(jnp.float32)
            for step in (1, 2, 3):
                total = total + plane_in[planes[step], :, columns].astype(jnp.float32)
            out[:, columns] = total.astype(jnp.bfloat16)

        over_piece(h, finish)

    for copy in sent:
        copy.wait_send()
    for step in range(PLANES):
        for h in range(PIECES):
            pass_on(planes[step], h, lambda copy: copy.wait_send())


def gathered(tokens, expert_ids, gate_weights, w_gate, w_up, w_down):
    tok_rows, width = tokens.shape
    hidden_units = w_down.shape[1]
    pair = 2 * capacity_of(tok_rows, expert_ids.shape[1], DEVICES // 2)
    full, wide = 2 * tok_rows, width + LANES
    any_spec = pl.BlockSpec(memory_space=pl.ANY)
    vmem_spec = pl.BlockSpec(memory_space=pltpu.VMEM)
    bf16, dma = jnp.bfloat16, pltpu.SemaphoreType.DMA
    return pl.pallas_call(
        gathered_kernel,
        out_shape=jax.ShapeDtypeStruct((tok_rows, width), bf16),
        in_specs=[any_spec, vmem_spec, vmem_spec, any_spec, any_spec, any_spec],
        out_specs=vmem_spec,
        scratch_shapes=[
            pltpu.VMEM((PLANES, 2, full + pair, wide), bf16),
            pltpu.VMEM((width, hidden_units), bf16),
            pltpu.VMEM((width, hidden_units), bf16),
            pltpu.VMEM((hidden_units, width), bf16),
            pltpu.VMEM((PLANES, pair, wide), bf16),
            pltpu.VMEM((PLANES, full, pair), bf16),
            pltpu.VMEM((PLANES, 2, full + pair, width), bf16),
            pltpu.VMEM((PLANES, full + pair, width), bf16),
            pltpu.VMEM((PLANES, pair, width), bf16),
            pltpu.VMEM((PLANES, pair, width), bf16),
            pltpu.VMEM((PLANES, tok_rows, width), bf16),
            pltpu.VMEM((PLANES, tok_rows, width), bf16),
            pltpu.VMEM((PLANES, tok_rows, width), bf16),
            pltpu.VMEM((PLANES, tok_rows, width), bf16),
            pltpu.VMEM((PLANES, tok_rows, width), jnp.float32),
            pltpu.VMEM((2 * (full + pair), hidden_units), bf16),
        ]
        + [dma((PLANES,))]
        + [dma((PLANES, PIECES))] * 19,
        compiler_params=pltpu.CompilerParams(
            collective_id=0, has_side_effects=True, vmem_limit_bytes=60 * 1024 * 1024
        ),
        cost_estimate=pl.CostEstimate(
            flops=6 * DEVICES * tok_rows * width * hidden_units,
            bytes_accessed=6 * width * hidden_units,
            transcendentals=DEVICES * tok_rows * hidden_units,
        ),
    )(tokens, expert_ids.T, gate_weights.T, w_gate, w_up, w_down)


def expert_block(w_gate, w_up, w_down, received):
    sources, count, width = received.shape
    flattened = received.reshape(sources * count, width)
    gate_value = jnp.dot(flattened, w_gate[0], preferred_element_type=jnp.float32)
    up_value = jnp.dot(flattened, w_up[0], preferred_element_type=jnp.float32)
    hidden = (jax.nn.silu(gate_value) * up_value).astype(jnp.bfloat16)
    partial_out = jnp.dot(hidden, w_down[0], preferred_element_type=jnp.float32).astype(
        jnp.bfloat16
    )
    return partial_out.reshape(sources, count, width)


def exchanged(tokens, expert_ids, gate_weights, w_gate, w_up, w_down):
    devices = lax.axis_size("expert")
    experts = devices // 2
    tok_rows, width = tokens.shape
    chosen_count = expert_ids.shape[1]
    capacity = capacity_of(tok_rows, chosen_count, experts)
    one_hot = (expert_ids[:, :, None] == jnp.arange(experts, dtype=jnp.int32)).astype(jnp.int32)
    per_row = jnp.sum(one_hot, axis=1)
    earlier = jnp.cumsum(per_row, axis=0) - per_row
    slot_index = jnp.sum(one_hot * earlier[:, None, :], axis=2)
    position = expert_ids * capacity + slot_index
    row_index = jnp.broadcast_to(jnp.arange(tok_rows, dtype=jnp.int32)[:, None], expert_ids.shape)
    owner = (
        jnp.full((experts * capacity,), tok_rows, jnp.int32)
        .at[position.reshape(-1)]
        .set(row_index.reshape(-1))
    )
    padded = jnp.concatenate([tokens, jnp.zeros((1, width), tokens.dtype)], axis=0)
    selected = padded[owner].reshape(experts, 1, capacity, width)
    outgoing = jnp.broadcast_to(selected, (experts, 2, capacity, width)).reshape(
        devices, capacity, width
    )
    partial_out = expert_block(
        w_gate,
        w_up,
        w_down,
        lax.all_to_all(outgoing, "expert", split_axis=0, concat_axis=0, tiled=True),
    )
    returned = lax.all_to_all(partial_out, "expert", split_axis=0, concat_axis=0, tiled=True)
    paired = returned.reshape(experts, 2, capacity, width).astype(jnp.float32)
    expert_out = (paired[:, 0] + paired[:, 1]).astype(jnp.bfloat16)
    picked = expert_out.reshape(experts * capacity, width)[position]
    mixed = jnp.sum(gate_weights[:, :, None] * picked.astype(jnp.float32), axis=1)
    return mixed.astype(jnp.bfloat16)


def solution(mesh):
    small = mesh.shape["expert"] == DEVICES and mesh.shape["groups"] == 1
    return jax.shard_map(
        gathered if small else exchanged,
        mesh=mesh,
        in_specs=(
            P(("groups", "expert"), None),
            P(("groups", "expert"), None),
            P(("groups", "expert"), None),
            P("expert", None, None),
            P("expert", None, None),
            P("expert", None, None),
        ),
        out_specs=P(("groups", "expert"), None),
        check_vma=False,
    )
```

```python
import jax
import jax.numpy as jnp
from jax import lax
from jax.experimental import pallas as pl
from jax.experimental.pallas import tpu as pltpu
from jax.sharding import PartitionSpec as P

LANES = 128
PLANES = 4
DEVICES = PLANES * 4 * 2
TILE = 512
PIECES = 2


def capacity_of(tok_rows, chosen_count, experts):
    return min(tok_rows, 3 * tok_rows * chosen_count // (2 * experts))


def gathered_kernel(
    tokens, expert_ids, gate_weights, w_gate, w_up, w_down, out,
    rows, gate_mem, up_mem, down_mem, packed, chosen, parts, parts_in,
    second_out, second_in, first_out, first_in, plane_out, plane_in, kept, hidden_mem,
    load_sem, up_send, down_send, plane_recv, first_send, first_recv, second_send, second_recv,
    near_send, near_recv, far_send, far_recv, parts_send, parts_recv,
    back_second_send, back_second_recv, back_first_send, back_first_recv,
    back_plane_send, back_plane_recv,
):
    tok_rows, width = tokens.shape
    wide = width + LANES
    experts = DEVICES // 2
    capacity = capacity_of(tok_rows, expert_ids.shape[0], experts)
    full, pair = 2 * tok_rows, 2 * capacity
    me = lax.axis_index("expert")
    core = lax.rem(me, 2)
    x = lax.rem(me // 2, 2)
    y = lax.rem(me // 4, 2)
    z = me // 8
    expert = me // 2
    along_x, along_y = me + 2 - 4 * x, me + 4 - 8 * y
    first = along_x * (1 - core) + along_y * core
    second = along_y * (1 - core) + along_x * core
    sibling = me + 1 - 2 * core
    above, below = lax.rem(me + 8, DEVICES), lax.rem(me + 24, DEVICES)

    half = z // 2
    low = z + half * (3 - 2 * z)
    planes = [z] + [t + half * (3 - 2 * t) for t in (low + 1, 2 - 2 * low, 3)]

    def remote(src, dst, send, recv, device):
        return pltpu.make_async_remote_copy(
            src_ref=src, dst_ref=dst, send_sem=send, recv_sem=recv,
            device_id={"expert": device}, device_id_type=pl.DeviceIdType.MESH,
        )

    sent = []

    def send(copy):
        copy.start()
        sent.append(copy)

    own = pl.ds(0, tok_rows)
    share_of_width = width // PIECES

    def wide_piece(h):
        return pl.ds(width - share_of_width, share_of_width + LANES) if h == 0 else plain_piece(h)

    def plain_piece(h):
        return pl.ds(width - share_of_width * (h + 1), share_of_width)

    def over_piece(h, body):
        @pl.loop(0, share_of_width // TILE)
        def _(j):
            start = width - share_of_width * (h + 1)
            body(pl.ds(pl.multiple_of(start + j * TILE, TILE), TILE))

    loads = [
        pltpu.make_async_copy(tokens, rows.at[z, core, own, pl.ds(0, width)], load_sem.at[0]),
        pltpu.make_async_copy(w_gate.at[0], gate_mem, load_sem.at[1]),
        pltpu.make_async_copy(w_up.at[0], up_mem, load_sem.at[2]),
        pltpu.make_async_copy(w_down.at[0], down_mem, load_sem.at[3]),
    ]
    for load in loads:
        load.start()

    barrier = pltpu.get_barrier_semaphore()
    partners = [lax.rem(me + 8 * step, DEVICES) for step in (1, 2, 3)] + [first, second, sibling]
    for partner in partners:
        pl.semaphore_signal(
            barrier, inc=1, device_id={"expert": partner}, device_id_type=pl.DeviceIdType.MESH
        )

    ids = jnp.transpose(expert_ids[...])
    gates = jnp.transpose(gate_weights[...])
    lane = lax.broadcasted_iota(jnp.int32, (tok_rows, LANES), 1)
    named = lax.rem(lane, experts)
    weight = jnp.zeros((tok_rows, LANES), jnp.float32)
    member = jnp.zeros((tok_rows, LANES), jnp.float32)
    for k in range(ids.shape[1]):
        same = ids[:, k : k + 1] == named
        weight += jnp.where(same, gates[:, k : k + 1], 0.0)
        member += jnp.where(same, 1.0, 0.0)
    earlier = lax.broadcasted_iota(jnp.int32, (tok_rows, tok_rows), 1) < lax.broadcasted_iota(
        jnp.int32, (tok_rows, tok_rows), 0
    )
    before = jnp.dot(
        jnp.where(earlier, 1.0, 0.0).astype(jnp.bfloat16),
        member.astype(jnp.bfloat16),
        preferred_element_type=jnp.float32,
    )
    high = weight.astype(jnp.bfloat16).astype(jnp.float32)
    beside = jnp.where(lane < experts, high, weight - high)
    beside = jnp.where(lane < 2 * experts, beside, member * (before + 1.0))
    rows[z, core, 0:tok_rows, width:wide] = jnp.where(lane < 3 * experts, beside, 0.0).astype(
        jnp.bfloat16
    )

    loads[0].wait()
    pl.semaphore_wait(barrier, len(partners))

    def column(shares, which):
        at = lax.broadcasted_iota(jnp.int32, shares.shape, 1)
        keep = at == which[0]
        for other in which[1:]:
            keep = keep | (at == other)
        return jnp.sum(jnp.where(keep, shares.astype(jnp.float32), 0.0), axis=1, keepdims=True)

    def plane_copy(q, h, up):
        block = rows.at[q, core, own, wide_piece(h)]
        sems = up_send if up else down_send
        return remote(block, block, sems.at[q, h], plane_recv.at[q, h], above if up else below)

    def pass_on(q, h, act):
        @pl.when((q <= z) & (z < PLANES - 1))
        def _():
            act(plane_copy(q, h, True))

        @pl.when((q >= z) & (z > 0))
        def _():
            act(plane_copy(q, h, False))

    def first_copy(q, h):
        return remote(
            rows.at[q, core, own, wide_piece(h)],
            rows.at[q, core, pl.ds(tok_rows, tok_rows), wide_piece(h)],
            first_send.at[q, h], first_recv.at[q, h], first,
        )

    def second_copy(q, h):
        return remote(
            packed.at[q, :, wide_piece(h)], rows.at[q, core, pl.ds(full, pair), wide_piece(h)],
            second_send.at[q, h], second_recv.at[q, h], second,
        )

    def near_copy(q, h, c):
        block = rows.at[q, c, pl.ds(0, full), wide_piece(h)]
        return remote(block, block, near_send.at[q, h], near_recv.at[q, h], sibling)

    def far_copy(q, h, c):
        block = rows.at[q, c, pl.ds(full, pair), wide_piece(h)]
        return remote(block, block, far_send.at[q, h], far_recv.at[q, h], sibling)

    inner = (z > 0) & (z < PLANES - 1)

    def gather_plane(step, h):
        q = planes[step]
        if step == 1:
            plane_copy(q, h, True).wait_recv()
        if step < 2:
            pass_on(q, h, lambda copy: copy.start())
        else:
            @pl.when(jnp.logical_not(inner))
            def _():
                plane_copy(q, h, True).wait_recv()

        send(first_copy(q, h))

    def gather_early(step, h):
        @pl.when(inner)
        def _():
            plane_copy(planes[step], h, True).wait_recv()
            pass_on(planes[step], h, lambda copy: copy.start())

    def gather_first(step, h):
        q = planes[step]
        first_copy(q, h).wait_recv()
        send(near_copy(q, h, core))
        if h == 0:
            code = column(rows[q, core, 0:full, width:wide], [2 * experts + second // 2])
            row = lax.broadcasted_iota(jnp.int32, (full, pair), 0)
            start = jnp.where(row < tok_rows, 0, capacity)
            place = code.astype(jnp.int32) - 1
            takes = (place >= 0) & (place + start == lax.broadcasted_iota(jnp.int32, (full, pair), 1))
            taken = jnp.where(takes, 1.0, 0.0).astype(jnp.bfloat16)
            chosen[step] = taken
        packed[q, :, wide_piece(h)] = lax.dot_general(
            chosen[step], rows[q, core, 0:full, wide_piece(h)], (((0,), (0,)), ((), ())),
            preferred_element_type=jnp.float32,
        ).astype(jnp.bfloat16)
        send(second_copy(q, h))

    def gather_second(step, h):
        q = planes[step]
        second_copy(q, h).wait_recv()
        send(far_copy(q, h, core))

    def parts_copy(step, h):
        return remote(
            parts.at[step, 1 - core, :, plain_piece(h)], parts_in.at[step, :, plain_piece(h)],
            parts_send.at[step, h], parts_recv.at[step, h], sibling,
        )

    def compute_hidden(step):
        q = planes[step]
        for h in range(PIECES):
            near_copy(q, h, 1 - core).wait_recv()
            far_copy(q, h, 1 - core).wait_recv()
        count = 2 * (full + pair)
        block = rows[q, :, :, 0:width].reshape(count, width)
        gate = jnp.dot(block, gate_mem[...], preferred_element_type=jnp.float32)
        up = jnp.dot(block, up_mem[...], preferred_element_type=jnp.float32)
        hidden_mem[...] = (gate / (1.0 + jnp.exp(-gate)) * up).astype(jnp.bfloat16)

    def compute_parts(step, h):
        def body(columns):
            part = jnp.dot(
                hidden_mem[...], down_mem[:, columns], preferred_element_type=jnp.float32
            )
            parts[step, :, :, columns] = part.astype(jnp.bfloat16).reshape(2, full + pair, TILE)

        over_piece(h, body)
        send(parts_copy(step, h))

    def share_of(step, start, size):
        shares = rows[planes[step], core, start : start + size, width:wide]
        return column(shares, [expert, expert + experts])

    def weighted(step, share, start, columns):
        at = pl.ds(start, share.shape[0])
        both = parts[step, core, at, columns].astype(jnp.float32) + parts_in[
            step, at, columns
        ].astype(jnp.float32)
        return share * both.astype(jnp.bfloat16).astype(jnp.float32)

    def back_second_copy(step, h):
        return remote(
            second_out.at[step, :, plain_piece(h)], second_in.at[step, :, plain_piece(h)],
            back_second_send.at[step, h], back_second_recv.at[step, h], second,
        )

    def back_first_copy(step, h):
        return remote(
            first_out.at[step, :, plain_piece(h)], first_in.at[step, :, plain_piece(h)],
            back_first_send.at[step, h], back_first_recv.at[step, h], first,
        )

    def reduce_parts(step, h):
        share = share_of(step, full, pair)
        parts_copy(step, h).wait_recv()

        def body(columns):
            second_out[step, :, columns] = weighted(step, share, full, columns).astype(jnp.bfloat16)

        over_piece(h, body)
        send(back_second_copy(step, h))

    def reduce_second(step, h):
        share = share_of(step, 0, full)
        back_second_copy(step, h).wait_recv()

        def body(columns):
            back = jnp.dot(
                chosen[step], second_in[step, :, columns], preferred_element_type=jnp.float32
            )
            total = weighted(step, share, 0, columns) + back
            first_out[step, :, columns] = total[tok_rows:].astype(jnp.bfloat16)
            kept[step, :, columns] = total[:tok_rows]

        over_piece(h, body)
        send(back_first_copy(step, h))

    def reduce_first(step, h):
        q = planes[step]
        back_first_copy(step, h).wait_recv()
        if step:

            def body(columns):
                plane_out[step, :, columns] = (
                    kept[step, :, columns] + first_in[step, :, columns].astype(jnp.float32)
                ).astype(jnp.bfloat16)

            over_piece(h, body)
            send(
                remote(
                    plane_out.at[step, :, plain_piece(h)], plane_in.at[z, :, plain_piece(h)],
                    back_plane_send.at[step, h], back_plane_recv.at[z, h],
                    lax.rem(me + 8 * (q - z) + DEVICES, DEVICES),
                )
            )

    gather_plane(0, 0)
    gather_plane(0, 1)
    gather_first(0, 0)
    gather_first(0, 1)
    gather_plane(1, 0)
    gather_early(2, 0)
    gather_plane(1, 1)
    gather_early(2, 1)
    gather_first(1, 0)
    gather_first(1, 1)
    gather_second(0, 0)
    gather_second(0, 1)
    for load in loads[1:]:
        load.wait()
    gather_plane(2, 0)
    gather_plane(2, 1)
    gather_early(3, 0)
    gather_early(3, 1)
    gather_first(2, 0)
    gather_first(2, 1)
    gather_second(1, 0)
    gather_second(1, 1)
    compute_hidden(1)
    gather_plane(3, 0)
    gather_plane(3, 1)
    compute_parts(1, 0)
    compute_parts(1, 1)
    gather_first(3, 0)
    gather_first(3, 1)
    gather_second(2, 0)
    gather_second(2, 1)
    reduce_parts(1, 0)
    reduce_parts(1, 1)
    compute_hidden(2)
    compute_parts(2, 0)
    compute_parts(2, 1)
    gather_second(3, 0)
    gather_second(3, 1)
    reduce_parts(2, 0)
    reduce_parts(2, 1)
    reduce_second(1, 0)
    reduce_second(1, 1)
    compute_hidden(3)
    compute_parts(3, 0)
    reduce_parts(3, 0)
    compute_parts(3, 1)
    reduce_parts(3, 1)
    reduce_first(1, 0)
    reduce_first(1, 1)
    compute_hidden(0)
    compute_parts(0, 0)
    compute_parts(0, 1)
    reduce_second(2, 0)
    reduce_second(2, 1)
    reduce_parts(0, 0)
    reduce_parts(0, 1)
    reduce_second(3, 0)
    reduce_second(3, 1)
    reduce_first(2, 0)
    reduce_first(2, 1)
    reduce_second(0, 0)
    reduce_first(3, 0)
    reduce_second(0, 1)
    reduce_first(3, 1)
    reduce_first(0, 0)
    reduce_first(0, 1)

    for h in range(PIECES):
        for step in (1, 2, 3):
            q = planes[step]
            remote(
                plane_out.at[step, :, plain_piece(h)], plane_in.at[q, :, plain_piece(h)],
                back_plane_send.at[step, h], back_plane_recv.at[q, h], sibling,
            ).wait_recv()

        def finish(columns):
            total = kept[0, :, columns] + first_in[0, :, columns].astype(jnp.float32)
            for step in (1, 2, 3):
                total = total + plane_in[planes[step], :, columns].astype(jnp.float32)
            out[:, columns] = total.astype(jnp.bfloat16)

        over_piece(h, finish)

    for copy in sent:
        copy.wait_send()
    for step in range(PLANES):
        for h in range(PIECES):
            pass_on(planes[step], h, lambda copy: copy.wait_send())


def gathered(tokens, expert_ids, gate_weights, w_gate, w_up, w_down):
    tok_rows, width = tokens.shape
    hidden_units = w_down.shape[1]
    pair = 2 * capacity_of(tok_rows, expert_ids.shape[1], DEVICES // 2)
    full, wide = 2 * tok_rows, width + LANES
    any_spec = pl.BlockSpec(memory_space=pl.ANY)
    vmem_spec = pl.BlockSpec(memory_space=pltpu.VMEM)
    bf16, dma = jnp.bfloat16, pltpu.SemaphoreType.DMA
    return pl.pallas_call(
        gathered_kernel,
        out_shape=jax.ShapeDtypeStruct((tok_rows, width), bf16),
        in_specs=[any_spec, vmem_spec, vmem_spec, any_spec, any_spec, any_spec],
        out_specs=vmem_spec,
        scratch_shapes=[
            pltpu.VMEM((PLANES, 2, full + pair, wide), bf16),
            pltpu.VMEM((width, hidden_units), bf16),
            pltpu.VMEM((width, hidden_units), bf16),
            pltpu.VMEM((hidden_units, width), bf16),
            pltpu.VMEM((PLANES, pair, wide), bf16),
            pltpu.VMEM((PLANES, full, pair), bf16),
            pltpu.VMEM((PLANES, 2, full + pair, width), bf16),
            pltpu.VMEM((PLANES, full + pair, width), bf16),
            pltpu.VMEM((PLANES, pair, width), bf16),
            pltpu.VMEM((PLANES, pair, width), bf16),
            pltpu.VMEM((PLANES, tok_rows, width), bf16),
            pltpu.VMEM((PLANES, tok_rows, width), bf16),
            pltpu.VMEM((PLANES, tok_rows, width), bf16),
            pltpu.VMEM((PLANES, tok_rows, width), bf16),
            pltpu.VMEM((PLANES, tok_rows, width), jnp.float32),
            pltpu.VMEM((2 * (full + pair), hidden_units), bf16),
        ]
        + [dma((PLANES,))]
        + [dma((PLANES, PIECES))] * 19,
        compiler_params=pltpu.CompilerParams(
            collective_id=0, has_side_effects=True, vmem_limit_bytes=60 * 1024 * 1024
        ),
        cost_estimate=pl.CostEstimate(
            flops=6 * DEVICES * tok_rows * width * hidden_units,
            bytes_accessed=6 * width * hidden_units,
            transcendentals=DEVICES * tok_rows * hidden_units,
        ),
    )(tokens, expert_ids.T, gate_weights.T, w_gate, w_up, w_down)


def expert_block(w_gate, w_up, w_down, received):
    sources, count, width = received.shape
    flattened = received.reshape(sources * count, width)
    gate_value = jnp.dot(flattened, w_gate[0], preferred_element_type=jnp.float32)
    up_value = jnp.dot(flattened, w_up[0], preferred_element_type=jnp.float32)
    hidden = (jax.nn.silu(gate_value) * up_value).astype(jnp.bfloat16)
    partial_out = jnp.dot(hidden, w_down[0], preferred_element_type=jnp.float32).astype(
        jnp.bfloat16
    )
    return partial_out.reshape(sources, count, width)


def exchanged(tokens, expert_ids, gate_weights, w_gate, w_up, w_down):
    devices = lax.axis_size("expert")
    experts = devices // 2
    tok_rows, width = tokens.shape
    chosen_count = expert_ids.shape[1]
    capacity = capacity_of(tok_rows, chosen_count, experts)
    one_hot = (expert_ids[:, :, None] == jnp.arange(experts, dtype=jnp.int32)).astype(jnp.int32)
    per_row = jnp.sum(one_hot, axis=1)
    earlier = jnp.cumsum(per_row, axis=0) - per_row
    slot_index = jnp.sum(one_hot * earlier[:, None, :], axis=2)
    position = expert_ids * capacity + slot_index
    row_index = jnp.broadcast_to(jnp.arange(tok_rows, dtype=jnp.int32)[:, None], expert_ids.shape)
    owner = (
        jnp.full((experts * capacity,), tok_rows, jnp.int32)
        .at[position.reshape(-1)]
        .set(row_index.reshape(-1))
    )
    padded = jnp.concatenate([tokens, jnp.zeros((1, width), tokens.dtype)], axis=0)
    selected = padded[owner].reshape(experts, 1, capacity, width)
    outgoing = jnp.broadcast_to(selected, (experts, 2, capacity, width)).reshape(
        devices, capacity, width
    )
    partial_out = expert_block(
        w_gate,
        w_up,
        w_down,
        lax.all_to_all(outgoing, "expert", split_axis=0, concat_axis=0, tiled=True),
    )
    returned = lax.all_to_all(partial_out, "expert", split_axis=0, concat_axis=0, tiled=True)
    paired = returned.reshape(experts, 2, capacity, width).astype(jnp.float32)
    expert_out = (paired[:, 0] + paired[:, 1]).astype(jnp.bfloat16)
    picked = expert_out.reshape(experts * capacity, width)[position]
    mixed = jnp.sum(gate_weights[:, :, None] * picked.astype(jnp.float32), axis=1)
    return mixed.astype(jnp.bfloat16)


def solution(mesh):
    small = mesh.shape["expert"] == DEVICES and mesh.shape["groups"] == 1
    return jax.shard_map(
        gathered if small else exchanged,
        mesh=mesh,
        in_specs=(
            P(("groups", "expert"), None),
            P(("groups", "expert"), None),
            P(("groups", "expert"), None),
            P("expert", None, None),
            P("expert", None, None),
            P("expert", None, None),
        ),
        out_specs=P(("groups", "expert"), None),
        check_vma=False,
    )
```
